32 devices in a mesh: scenes: 2 (over x), rows: 16 (over z, y, core).
Axes of the slice: x: 2, y: 2, z: 4, core: 2. Of those that a mesh axis runs over, the one named last changes fastest.
Arguments:
- images: float32 [64, 128, 128], P(('scenes', 'rows')), parts along dimension 0, may hold values from -6 to 6
- conv_weight: float32 [3, 3, 128, 128], replicated, may hold values from -0.1875 to 0.1875
- lift_weight: float32 [320, 128], replicated, may hold values from -0.5 to 0.5
- vol_weight: float32 [3, 3, 3, 32, 40], replicated, may hold values from -0.1875 to 0.1875
Outputs:
- filtered: float32 [64, 32, 48, 128], P(('scenes', 'rows')), parts along dimension 0
The draws below stay inside these ranges and needn't reach their ends.
There are 2 independent parts, one for each index of `scenes`. The reference program is written for one: setup_inputs(seed, part) draws one part's arguments, and reference() takes and returns one part's arrays. A program takes and returns all parts, laid end to end along the dimension named above; an argument that names none is the same for every part. Nothing has to cross between parts.
All inputs are finite; a program needn't handle non-finite values.
Results may differ from the reference program's by a relative error of at most 0.0001.
Values sent between devices are 32-bit elements; how exact they have to be, the bound alone decides.
No kernel may reach another device: no remote copies, remote signals or barrier semaphores. Data moves between devices by JAX's collectives and lax.ppermute only.
A program may use at most 128 MiB of HBM per device.

```python
import jax
import jax.numpy as jnp
from jax import lax

CIN = 128
FEAT = 320
GROUPS = 40
DISP = 48
OUTC = 32
COLS = 128
HEIGHT = 16


def block_scale(stream_key, dims, pieces, least, largest):
    factor_of = 1.0
    for position, blocks in pieces:
        heights = jax.random.uniform(jax.random.fold_in(jax.random.fold_in(stream_key, 6), position), (blocks,), jnp.float32, least / len(pieces), largest / len(pieces))
        factor_of = factor_of * jnp.repeat(jnp.exp(heights), dims[position] // blocks).reshape((-1,) + (1,) * (len(dims) - 1 - position))
    return factor_of


def centred(rng, shape, spread, most, split=(), dtype=jnp.bfloat16):
    factor_of = block_scale(rng, shape, split, -0.22, 0.18) if split else 1.0
    array = jax.random.normal(rng, shape, jnp.float32) * spread * factor_of
    return jnp.minimum(jnp.maximum(array, -most), most).astype(dtype)


def setup_inputs(seed: int = 0, part: int = 0) -> dict:
    seeds = jax.random.split(jax.random.key(seed), 5)
    own_keys = jax.random.split(jax.random.fold_in(seeds[4], part), 5)
    return {
        "images": centred(own_keys[0], (2 * HEIGHT, CIN, COLS), 1.0, 6.0, ((0, 16),), jnp.float32),
        "conv_weight": centred(seeds[1], (3, 3, CIN, CIN), (9 * CIN) ** -0.5, 0.1875, (), jnp.float32),
        "lift_weight": centred(seeds[2], (FEAT, CIN), CIN ** -0.5, 0.5, (), jnp.float32),
        "vol_weight": centred(seeds[3], (3, 3, 3, OUTC, GROUPS), (27 * GROUPS) ** -0.5, 0.1875, (), jnp.float32),
    }


precise = lax.Precision.HIGHEST


def conv_plane(planes, weight, padding):
    result = lax.conv_general_dilated(planes[None], weight, (1, 1), padding, dimension_numbers=("NHCW", "HWOI", "NHCW"), precision=precise)
    return result[0]


def lift_features(weight, hidden):
    return jnp.einsum("fi,ric->rfc", weight, hidden, precision=precise)


def correlate(anchor, other, groups, disparities):
    row_count, channels, columns = anchor.shape
    padded = jnp.pad(other, ((0, 0), (0, 0), (disparities, 0)))
    layers = []
    for offset in range(disparities):
        shifted = padded[:, :, disparities - offset:disparities - offset + columns]
        product = (anchor * shifted).reshape(row_count, groups, channels // groups, columns)
        layers.append(jnp.mean(product, axis=2))
    return jnp.stack(layers, axis=2)


def conv_volume(volume, weight, padding):
    result = lax.conv_general_dilated(volume[None], weight, (1, 1, 1), padding, dimension_numbers=("NHCDW", "HDWOI", "NHCDW"), precision=precise)
    return result[0]


def reference(images, conv_weight, lift_weight, vol_weight):
    middle = images.shape[0] // 2
    offset_rows = middle // 2
    unrolled = jnp.roll(images, -offset_rows, axis=0)
    left_feat = lift_features(lift_weight, jax.nn.relu(conv_plane(unrolled[:middle], conv_weight, ((1, 1), (1, 1)))))
    right_feat = lift_features(lift_weight, jax.nn.relu(conv_plane(unrolled[middle:], conv_weight, ((1, 1), (1, 1)))))
    left_cost = correlate(left_feat, right_feat, GROUPS, DISP)
    right_cost = jnp.flip(correlate(jnp.flip(right_feat, -1), jnp.flip(left_feat, -1), GROUPS, DISP), -1)
    padding = ((1, 1), (1, 1), (1, 1))
    joined = jnp.concatenate([conv_volume(left_cost, vol_weight, padding), conv_volume(right_cost, vol_weight, padding)], axis=0)
    return jnp.roll(joined, offset_rows, axis=0)
```

```python
import functools

import jax
import jax.numpy as jnp
from jax import lax
from jax.experimental import pallas as pl
from jax.experimental.pallas import tpu as pltpu
from jax.sharding import PartitionSpec as P

GROUPS = 40
DISP = 48
F32 = jnp.float32
BF16 = jnp.bfloat16
VMEM_BYTES = 48 * 1024 * 1024


def split(x):
    high = x.astype(BF16)
    return high, (x - high.astype(F32)).astype(BF16)


def split_outside(x):
    high = lax.reduce_precision(x, 8, 7)
    return high.astype(BF16), (x - high).astype(BF16)


def mm(a, b):
    return jnp.dot(a, b, preferred_element_type=F32)


def from_columns(y, size):
    column = lax.broadcasted_iota(jnp.int32, (size, y.shape[1]), 1)
    last = y.shape[1] - 1
    left = jnp.where(column > 0, pltpu.roll(y[:size], 1, 1), 0.0)
    right = jnp.where(column < last, pltpu.roll(y[2 * size :], last, 1), 0.0)
    return y[size : 2 * size] + left + right


def features_kernel(flags, own, mate, far, conv_high, conv_low, lift_high, lift_low, out, x_high, x_low):
    rows, channels, columns = own.shape
    edge = mate.shape[0]
    odd = flags[0]
    total = rows + 2 * edge

    def place(block, at):
        count = block.shape[0] * channels
        high, low = split(block[...].reshape(count, columns))
        x_high[pl.ds(pl.multiple_of(at * channels, channels), count)] = high
        x_low[pl.ds(pl.multiple_of(at * channels, channels), count)] = low

    place(own, edge)
    place(mate, jnp.where(odd == 1, 0, total - edge))
    place(far, jnp.where(odd == 1, total - edge, 0))
    depth = 3 * channels
    feats = lift_high.shape[0]
    for row in range(0, rows + 2, 2):
        starts = [(row + k) * channels for k in range(2)]
        high = jnp.concatenate([x_high[s : s + depth] for s in starts], axis=1)
        low = jnp.concatenate([x_low[s : s + depth] for s in starts], axis=1)
        y = mm(conv_high[...], high) + (mm(conv_low[...], high) + mm(conv_high[...], low))
        hidden = []
        for k in range(2):
            h = jnp.maximum(from_columns(y[:, k * columns : (k + 1) * columns], channels), 0.0)
            if row + k == 0:
                h = h * flags[1].astype(F32)
            if row + k == rows + 1:
                h = h * flags[2].astype(F32)
            hidden.append(h)
        high, low = split(jnp.concatenate(hidden, axis=1))
        f = mm(lift_high[...], high) + (mm(lift_low[...], high) + mm(lift_high[...], low))
        for k in range(2):
            out[(row + k) * feats : (row + k + 1) * feats] = f[:, k * columns : (k + 1) * columns]


def volume_kernel(flags, anchor, other, weight, out, cost, c_high, c_low, *, rows, outs):
    columns = anchor.shape[1]
    slab = (rows + 2) * GROUPS
    per = anchor.shape[0] // slab
    right = flags[3] == 1
    column = lax.broadcasted_iota(jnp.int32, (8, columns), 1)
    place = jnp.where(right, columns - 1 - column, column)
    cost[:slab] = jnp.zeros((slab, columns), F32)
    cost[(DISP + 1) * slab :] = jnp.zeros((slab, columns), F32)

    def correlate(i, carry):
        at = pl.ds(pl.multiple_of(i * 8 * per, 8 * per), 8 * per)
        a = anchor[at]
        b = other[at]
        for d in range(DISP):
            shifted = pltpu.roll(b, jnp.where(right, columns - d, d), 1) if d else b
            c = jnp.sum((a * shifted).reshape(per, 8, columns), axis=0)
            if d:
                c = jnp.where(place >= d, c, 0.0)
            cost[pl.ds(pl.multiple_of((d + 1) * slab + i * 8, 8), 8)] = c
        return carry

    lax.fori_loop(0, slab // 8, correlate, 0)

    def halve(d, carry):
        at = pl.ds(pl.multiple_of(d * slab, slab), slab)
        high, low = split(cost[at])
        c_high[at] = high
        c_low[at] = low
        return carry

    lax.fori_loop(0, DISP + 2, halve, 0)
    m = 3 * rows * outs

    def filter_two(q, carry):
        base = q * 2 * slab
        ats = [pl.ds(pl.multiple_of(base + k * slab, slab), 3 * slab) for k in range(2)]
        high = jnp.concatenate([c_high[at] for at in ats], axis=1)
        low = jnp.concatenate([c_low[at] for at in ats], axis=1)
        y = mm(weight[...], high)
        y = y[:m] + (y[m:] + mm(weight[:m], low))
        for k in range(2):
            o = from_columns(y[:, k * columns : (k + 1) * columns], rows * outs)
            out[pl.ds(2 * q + k, rows * outs, stride=DISP)] = o
        return carry

    lax.fori_loop(0, DISP // 2, filter_two, 0)


def vmem():
    return pl.BlockSpec(memory_space=pltpu.VMEM)


def smem():
    return pl.BlockSpec(memory_space=pltpu.SMEM)


def features(flags, own, mate, far, conv, lift):
    rows, channels, columns = own.shape
    total = (rows + 2 * mate.shape[0]) * channels
    return pl.pallas_call(
        features_kernel,
        out_shape=jax.ShapeDtypeStruct(((rows + 2) * lift[0].shape[0], columns), F32),
        in_specs=[smem()] + [vmem()] * 7,
        out_specs=vmem(),
        scratch_shapes=[pltpu.VMEM((total, columns), BF16)] * 2,
        compiler_params=pltpu.CompilerParams(vmem_limit_bytes=VMEM_BYTES),
        name="features",
    )(flags, own, mate, far, *conv, *lift)


def volumes(flags, anchor, other, weight, rows, outs):
    columns = anchor.shape[1]
    depth = (DISP + 2) * (rows + 2) * GROUPS
    return pl.pallas_call(
        functools.partial(volume_kernel, rows=rows, outs=outs),
        out_shape=jax.ShapeDtypeStruct((rows * outs * DISP, columns), F32),
        in_specs=[smem()] + [vmem()] * 3,
        out_specs=vmem(),
        scratch_shapes=[pltpu.VMEM((depth, columns), F32), pltpu.VMEM((depth, columns), BF16), pltpu.VMEM((depth, columns), BF16)],
        compiler_params=pltpu.CompilerParams(vmem_limit_bytes=VMEM_BYTES),
        name="volumes",
    )(flags, anchor, other, weight)


def conv_operand(weight):
    outs, ins = weight.shape[2:]
    return split_outside(weight.transpose(1, 2, 0, 3).reshape(3 * outs, 3 * ins))


def lift_operand(weight):
    feats, ins = weight.shape
    per = feats // GROUPS
    ordered = weight.reshape(GROUPS // 8, 8, per, ins).transpose(0, 2, 1, 3)
    return split_outside(ordered.reshape(feats, ins))


def volume_operand(weight, rows, per):
    outs, groups = weight.shape[3:]
    taps = (weight * (1.0 / per)).transpose(2, 3, 1, 0, 4).reshape(3, outs, 3, 3 * groups)
    banded = [jnp.pad(taps, ((0, 0), (0, 0), (0, 0), (r * groups, (rows - 1 - r) * groups))) for r in range(rows)]
    whole = jnp.stack(banded, axis=1).reshape(3 * rows * outs, 3 * (rows + 2) * groups)
    return jnp.concatenate(split_outside(whole), axis=0)


def neighbours(size, quarter):
    def across(i):
        return (i + 1) % size if i % 2 else (i - 1) % size

    def apart(i):
        low, high = min(i, across(i)), max(i, across(i))
        return high - low == 1 and high in (quarter, 3 * quarter)

    mates = [(i, i ^ 1) for i in range(size)]
    far = [(i, across(i)) for i in range(size) if not apart(i)]
    return mates, far


def on_device(images, conv_weight, lift_weight, vol_weight):
    size = lax.axis_size("rows")
    position = lax.axis_index("rows")
    half, quarter = size // 2, size // 4
    rows = images.shape[0]
    odd = position % 2
    mates, far = neighbours(size, quarter)
    starts = (position == quarter) | (position == 3 * quarter)
    ends = (position == quarter - 1) | (position == 3 * quarter - 1)
    right = (position < quarter) | (position >= 3 * quarter)
    flags = jnp.stack([odd, jnp.where(starts, 0, 1), jnp.where(ends, 0, 1), jnp.where(right, 1, 0)]).astype(jnp.int32)

    def sent(x, to_first):
        if rows == 2:
            return x
        return jnp.where(to_first, x[:2], x[rows - 2 :])

    def framed(x):
        return lax.ppermute(sent(x, odd == 1), "rows", mates), lax.ppermute(sent(x, odd == 0), "rows", far)

    partner = lax.ppermute(images, "rows", [(i, (i + half) % size) for i in range(size)])
    conv = conv_operand(conv_weight)
    lift = lift_operand(lift_weight)
    per = lift_weight.shape[0] // GROUPS
    outs = vol_weight.shape[3]
    vol = volume_operand(vol_weight, rows, per)
    mine = features(flags, images, *framed(images), conv, lift)
    theirs = features(flags, partner, *framed(partner), conv, lift)
    result = volumes(flags, mine, theirs, vol, rows, outs)
    return result.reshape(rows, outs, DISP, images.shape[2])


def solution(mesh):
    return jax.shard_map(
        on_device,
        mesh=mesh,
        in_specs=(P(("scenes", "rows"), None, None), P(), P(), P()),
        out_specs=P(("scenes", "rows"), None, None, None),
        check_vma=False,
    )
```

```python
import jax
import jax.numpy as jnp
from jax import lax
from jax.experimental import pallas as pl
from jax.experimental.pallas import tpu as pltpu
from jax.sharding import PartitionSpec as P

GROUPS = 40
DISP = 48
STEP = 8
COST = 10**11
F32 = jnp.float32
BF16 = jnp.bfloat16
VMEM_BYTES = 24 * 1024 * 1024


def split(x):
    high = x.astype(BF16)
    return high, (x - high.astype(F32)).astype(BF16)


def mm(a, b):
    return jnp.dot(a, b, preferred_element_type=F32)


def from_columns(y, size):
    column = lax.broadcasted_iota(jnp.int32, (size, y.shape[1]), 1)
    last = y.shape[1] - 1
    left = jnp.where(column > 0, pltpu.roll(y[:size], 1, 1), 0.0)
    right = jnp.where(column < last, pltpu.roll(y[2 * size :], last, 1), 0.0)
    return y[size : 2 * size] + left + right


def features(x, operands, to, inside):
    conv_high, conv_low, lift_high, lift_low = operands
    channels = conv_high.shape[0] // 3
    columns = x.shape[2]
    feats = lift_high.shape[0]
    high, low = split(x.reshape(4 * channels, columns))
    at = [slice(k * channels, (k + 3) * channels) for k in range(2)]
    high = jnp.concatenate([high[s] for s in at], axis=1)
    low = jnp.concatenate([low[s] for s in at], axis=1)
    y = mm(conv_high[...], high) + (mm(conv_low[...], high) + mm(conv_high[...], low))
    hidden = []
    for k in range(2):
        h = jnp.maximum(from_columns(y[:, k * columns : (k + 1) * columns], channels), 0.0)
        hidden.append(jnp.where(inside[k], h, 0.0))
    high, low = split(jnp.concatenate(hidden, axis=1))
    f = mm(lift_high[...], high) + (mm(lift_low[...], high) + mm(lift_high[...], low))
    for k in range(2):
        to[k * feats : (k + 1) * feats] = f[:, k * columns : (k + 1) * columns]


def four_rows(half, block, beside):
    a, b = block[...], beside[...]
    first = half == 1
    return jnp.concatenate([jnp.where(first, a, b), jnp.where(first, b, a)], axis=0)


def rows_inside(flags, half):
    return [jnp.logical_or(half != k, flags[2 + k] == 1) for k in range(2)]


def prepare_kernel(flags, conv_hbm, lift_hbm, vol_hbm, own_hbm, mate, conv_high, conv_low, lift_high, lift_low, banded, anchor, conv, lift, vol, own, sems):
    pairs = ((conv_hbm, conv), (lift_hbm, lift), (vol_hbm, vol), (own_hbm, own))
    copies = [pltpu.make_async_copy(a, b, sems.at[i]) for i, (a, b) in enumerate(pairs)]
    for copy in copies:
        copy.start()
    channels = conv.shape[2]
    copies[0].wait()
    for dr in range(3):
        for dc in range(3):
            high, low = split(conv[dr, dc])
            at = (slice(dc * channels, (dc + 1) * channels), slice(dr * channels, (dr + 1) * channels))
            conv_high[at] = high
            conv_low[at] = low
    feats = lift.shape[0]
    per = feats // GROUPS
    copies[1].wait()
    for g in range(0, feats, 8 * per):
        ordered = jnp.concatenate([lift[pl.ds(g + j, 8, stride=per)] for j in range(per)], axis=0)
        high, low = split(ordered)
        lift_high[g : g + 8 * per] = high
        lift_low[g : g + 8 * per] = low
    outs = vol.shape[3]
    m = 3 * outs
    nothing = jnp.zeros((m, GROUPS), F32)
    copies[2].wait()
    for half in range(2):
        for row in range(2):
            pieces = []
            for dd in range(3):
                for place in range(2):
                    dr = 2 * half + place - row
                    pieces.append(vol[dr, dd].reshape(m, GROUPS) * (1.0 / per) if 0 <= dr < 3 else nothing)
            high, low = split(jnp.concatenate(pieces, axis=1))
            banded[(4 * half + row) * m : (4 * half + row + 1) * m] = high
            banded[(4 * half + 2 + row) * m : (4 * half + 3 + row) * m] = low
    half = 1 - flags[1]
    copies[3].wait()
    features(four_rows(half, own, mate), (conv_high, conv_low, lift_high, lift_low), anchor, rows_inside(flags, half))


def correlate(right, anchor, other, shifted, c_high, c_low, per):
    columns = anchor.shape[1]
    column = lax.broadcasted_iota(jnp.int32, (8, columns), 1)
    place = jnp.where(right, columns - 1 - column, column)

    def along(x, d):
        if d == 0:
            return x
        there, back = d % columns, -d % columns
        return pltpu.roll(x, jnp.where(right, back, there), 1)

    slab = 2 * GROUPS
    nothing = jnp.zeros((slab, columns), BF16)
    for c in (c_high, c_low):
        c[:slab] = nothing
        c[(DISP + 1) * slab :] = nothing
    block = 8 * per
    blocks = [slice(i * block, (i + 1) * block) for i in range(slab // 8)]
    for at in blocks:
        values = other[at]
        for b in range(1, STEP):
            shifted[b, at] = along(values, b)
    for a in range(0, DISP, STEP):
        for i in range(0, len(blocks), 2):
            moved = [along(anchor[at], -a) for at in blocks[i : i + 2]]
            for b in range(min(STEP, DISP - a)):
                d = a + b
                tiles = []
                for m, at in zip(moved, blocks[i : i + 2]):
                    c = jnp.sum((m * (shifted[b, at] if b else other[at])).reshape(per, 8, columns), axis=0)
                    c = along(c, a)
                    tiles.append(jnp.where(place >= d, c, 0.0) if d else c)
                high, low = split(jnp.concatenate(tiles, axis=0))
                at = slice((d + 1) * slab + i * 8, (d + 1) * slab + i * 8 + 16)
                c_high[at] = high
                c_low[at] = low


def filtered_pairs(half, banded, c_high, c_low):
    slab = 2 * GROUPS
    m = banded.shape[0] // 4
    weight = banded[pl.ds(pl.multiple_of(half * 2 * m, 2 * m), 2 * m)]
    for d in range(0, DISP, 2):
        at = [slice((d + k) * slab, (d + k + 3) * slab) for k in range(2)]
        high = jnp.concatenate([c_high[s] for s in at], axis=1)
        low = jnp.concatenate([c_low[s] for s in at], axis=1)
        y = mm(weight, high)
        yield d, y[:m] + (y[m:] + mm(weight[:m], low))


def near_kernel(flags, partner, mate, anchor, conv_high, conv_low, lift_high, lift_low, banded, out, other, shifted, c_high, c_low):
    half = 1 - flags[1]
    operands = (conv_high, conv_low, lift_high, lift_low)
    features(four_rows(half, partner, mate), operands, other, rows_inside(flags, half))
    per = lift_high.shape[0] // GROUPS
    correlate(flags[0] == 1, anchor, other, shifted, c_high, c_low, per)
    for d, y in filtered_pairs(half, banded, c_high, c_low):
        out[d // 2] = y


def far_kernel(flags, own, own_far, partner, partner_far, conv_high, conv_low, lift_high, lift_low, banded, part, out, anchor, other, shifted, c_high, c_low):
    half = flags[1]
    operands = (conv_high, conv_low, lift_high, lift_low)
    features(four_rows(half, partner, partner_far), operands, other, rows_inside(flags, half))
    features(four_rows(half, own, own_far), operands, anchor, rows_inside(flags, half))
    per = lift_high.shape[0] // GROUPS
    correlate(flags[0] == 1, anchor, other, shifted, c_high, c_low, per)
    columns = own.shape[2]
    outs = banded.shape[0] // 24
    for d, y in filtered_pairs(half, banded, c_high, c_low):
        y = y + part[d // 2]
        for k in range(2):
            for row in range(2):
                o = from_columns(y[row * 3 * outs : (row + 1) * 3 * outs, k * columns : (k + 1) * columns], outs)
                out[pl.ds(row * outs * DISP + d + k, outs, stride=DISP)] = o


def vmem():
    return pl.BlockSpec(memory_space=pltpu.VMEM)


def smem():
    return pl.BlockSpec(memory_space=pltpu.SMEM)


def call(kernel, name, out_shape, scratch, flags, *args, in_hbm=0):
    return pl.pallas_call(
        kernel,
        out_shape=out_shape,
        in_specs=[smem()] + [pl.BlockSpec(memory_space=pltpu.HBM)] * in_hbm + [vmem()] * (len(args) - in_hbm),
        out_specs=jax.tree.map(lambda _: vmem(), out_shape),
        scratch_shapes=scratch,
        compiler_params=pltpu.CompilerParams(vmem_limit_bytes=VMEM_BYTES),
        cost_estimate=pl.CostEstimate(flops=COST, bytes_accessed=COST, transcendentals=0),
        name=name,
    )(flags, *args)


def prepare(flags, conv, lift, vol, own, mate):
    channels, columns = own.shape[1:]
    feats = lift.shape[0]
    shapes = [(3 * channels, 3 * channels)] * 2 + [(feats, channels)] * 2 + [(8 * 3 * vol.shape[3], 6 * GROUPS)]
    out = [jax.ShapeDtypeStruct(s, BF16) for s in shapes] + [jax.ShapeDtypeStruct((2 * feats, columns), F32)]
    scratch = [pltpu.VMEM(x.shape, F32) for x in (conv, lift, vol, own)] + [pltpu.SemaphoreType.DMA((4,))]
    *operands, anchor = call(prepare_kernel, "prepare", out, scratch, flags, *[pltpu.with_memory_space_constraint(x, pltpu.HBM) for x in (conv, lift, vol, own)], mate, in_hbm=4)
    return operands, anchor


def volume_scratch(feats, columns):
    depth = (DISP + 2) * 2 * GROUPS
    return [pltpu.VMEM((2 * feats, columns), F32), pltpu.VMEM((STEP, 2 * feats, columns), F32)] + [pltpu.VMEM((depth, columns), BF16)] * 2


def near(flags, partner, mate, anchor, operands):
    columns = partner.shape[2]
    feats = operands[2].shape[0]
    out = jax.ShapeDtypeStruct((DISP // 2, operands[4].shape[0] // 4, 2 * columns), F32)
    return call(near_kernel, "near", out, volume_scratch(feats, columns), flags, partner, mate, anchor, *operands)


def far(flags, own, own_far, partner, partner_far, operands, part):
    columns = own.shape[2]
    feats = operands[2].shape[0]
    out = jax.ShapeDtypeStruct((2 * operands[4].shape[0] // 24 * DISP, columns), F32)
    scratch = [pltpu.VMEM((2 * feats, columns), F32)] + volume_scratch(feats, columns)
    return call(far_kernel, "far", out, scratch, flags, own, own_far, partner, partner_far, *operands, part)


def routes(size):
    half, quarter = size // 2, size // 4

    def across(i):
        return (i + 1) % size if i % 2 else (i - 1) % size

    def apart(i, j):
        low, high = min(i, j), max(i, j)
        return high - low == 1 and high in (quarter, 3 * quarter)

    every = range(size)
    swap = [(i, (i + half) % size) for i in every]
    mates = [(i, i ^ 1) for i in every if not apart(i, i ^ 1)]
    far = [(across(i), i) for i in every if not apart(i, across(i))]
    far_partner = [((i + half) % size, j) for i, j in far]
    return swap, mates, far, far_partner


def on_device(images, conv_weight, lift_weight, vol_weight):
    size = lax.axis_size("rows")
    position = lax.axis_index("rows")
    quarter = size // 4
    swap, mates, beyond, beyond_partner = routes(size)
    starts = (position == quarter) | (position == 3 * quarter)
    ends = (position == quarter - 1) | (position == 3 * quarter - 1)
    right = (position < quarter) | (position >= 3 * quarter)
    flags = jnp.stack([jnp.where(right, 1, 0), position % 2, jnp.where(starts, 0, 1), jnp.where(ends, 0, 1)]).astype(jnp.int32)

    partner = lax.ppermute(images, "rows", swap)
    partner_far = lax.ppermute(images, "rows", beyond_partner)
    own_mate = lax.ppermute(images, "rows", mates)
    own_far = lax.ppermute(images, "rows", beyond)
    partner_mate = lax.ppermute(partner, "rows", mates)
    operands, anchor = prepare(flags, conv_weight, lift_weight, vol_weight, images, own_mate)
    part = near(flags, partner, partner_mate, anchor, operands)
    whole = far(flags, images, own_far, partner, partner_far, operands, part)
    rows, _, columns = images.shape
    return whole.reshape(rows, vol_weight.shape[3], DISP, columns)


def solution(mesh):
    return jax.shard_map(
        on_device,
        mesh=mesh,
        in_specs=(P(("scenes", "rows"), None, None), P(), P(), P()),
        out_specs=P(("scenes", "rows"), None, None, None),
        check_vma=False,
    )
```

```python
import jax
import jax.numpy as jnp
from jax import lax
from jax.experimental import pallas as pl
from jax.experimental.pallas import tpu as pltpu
from jax.sharding import PartitionSpec as P

GROUPS = 40
DISP = 48
STEP = 8
COST = 10**11
F32 = jnp.float32
BF16 = jnp.bfloat16
VMEM_BYTES = 24 * 1024 * 1024


def split(x):
    high = x.astype(BF16)
    return high, (x - high.astype(F32)).astype(BF16)


def mm(a, b):
    return jnp.dot(a, b, preferred_element_type=F32)


def from_columns(y, size):
    column = lax.broadcasted_iota(jnp.int32, (size, y.shape[1]), 1)
    last = y.shape[1] - 1
    left = jnp.where(column > 0, pltpu.roll(y[:size], 1, 1), 0.0)
    right = jnp.where(column < last, pltpu.roll(y[2 * size :], last, 1), 0.0)
    return y[size : 2 * size] + left + right


def features(fours, operands, tos, inside):
    conv_high, conv_low, lift_high, lift_low = operands
    channels = conv_high.shape[0] // 3
    columns = fours[0].shape[2]
    feats = lift_high.shape[0]
    at = [slice(k * channels, (k + 3) * channels) for k in range(2)]
    products = []
    for x in fours:
        high, low = split(x.reshape(4 * channels, columns))
        high = jnp.concatenate([high[s] for s in at], axis=1)
        low = jnp.concatenate([low[s] for s in at], axis=1)
        products.append(mm(conv_high[...], high) + (mm(conv_low[...], high) + mm(conv_high[...], low)))
    halves = []
    for y in products:
        hidden = []
        for k in range(2):
            h = jnp.maximum(from_columns(y[:, k * columns : (k + 1) * columns], channels), 0.0)
            hidden.append(jnp.where(inside[k], h, 0.0))
        halves.append(split(jnp.concatenate(hidden, axis=1)))
    for (high, low), to in zip(halves, tos):
        f = mm(lift_high[...], high) + (mm(lift_low[...], high) + mm(lift_high[...], low))
        for k in range(2):
            to[k * feats : (k + 1) * feats] = f[:, k * columns : (k + 1) * columns]


def four_rows(half, block, beside):
    a, b = block[...], beside[...]
    first = half == 1
    return jnp.concatenate([jnp.where(first, a, b), jnp.where(first, b, a)], axis=0)


def rows_inside(flags, half):
    return [jnp.logical_or(half != k, flags[2 + k] == 1) for k in range(2)]


def prepare_kernel(conv_hbm, lift_hbm, vol_hbm, conv_high, conv_low, lift_high, lift_low, banded, conv, lift, vol, sems):
    pairs = ((conv_hbm, conv), (lift_hbm, lift), (vol_hbm, vol))
    copies = [pltpu.make_async_copy(a, b, sems.at[i]) for i, (a, b) in enumerate(pairs)]
    for copy in copies:
        copy.start()
    channels = conv.shape[2]
    copies[0].wait()
    for dr in range(3):
        for dc in range(3):
            high, low = split(conv[dr, dc])
            at = (slice(dc * channels, (dc + 1) * channels), slice(dr * channels, (dr + 1) * channels))
            conv_high[at] = high
            conv_low[at] = low
    feats = lift.shape[0]
    per = feats // GROUPS
    copies[1].wait()
    for g in range(0, feats, 8 * per):
        ordered = jnp.concatenate([lift[pl.ds(g + j, 8, stride=per)] for j in range(per)], axis=0)
        high, low = split(ordered)
        lift_high[g : g + 8 * per] = high
        lift_low[g : g + 8 * per] = low
    outs = vol.shape[3]
    m = 3 * outs
    nothing = jnp.zeros((m, GROUPS), F32)
    copies[2].wait()
    for half in range(2):
        for row in range(2):
            pieces = []
            for dd in range(3):
                for place in range(2):
                    dr = 2 * half + place - row
                    pieces.append(vol[dr, dd].reshape(m, GROUPS) * (1.0 / per) if 0 <= dr < 3 else nothing)
            high, low = split(jnp.concatenate(pieces, axis=1))
            banded[(4 * half + row) * m : (4 * half + row + 1) * m] = high
            banded[(4 * half + 2 + row) * m : (4 * half + 3 + row) * m] = low


def mover(right, columns):
    def along(x, d):
        if d == 0:
            return x
        there, back = d % columns, -d % columns
        return pltpu.roll(x, jnp.where(right, back, there), 1)

    return along


def blocks_of(per):
    block = 8 * per
    return [slice(i * block, (i + 1) * block) for i in range(2 * GROUPS // 8)]


def move_other(right, other, shifted, per):
    along = mover(right, other.shape[1])
    for at in blocks_of(per):
        values = other[at]
        for b in range(1, STEP):
            shifted[b - 1, at] = along(values, b)


def move_anchor(right, anchor, moved, per):
    along = mover(right, anchor.shape[1])
    for k, a in enumerate(range(STEP, DISP, STEP)):
        for at in blocks_of(per):
            moved[k, at] = along(anchor[at], -a)


def correlate(right, anchor, moved, other, shifted, c_high, c_low, per):
    columns = anchor.shape[1]
    along = mover(right, columns)
    column = lax.broadcasted_iota(jnp.int32, (8, columns), 1)
    place = jnp.where(right, columns - 1 - column, column)
    slab = 2 * GROUPS
    nothing = jnp.zeros((slab, columns), BF16)
    for c in (c_high, c_low):
        c[:slab] = nothing
        c[(DISP + 1) * slab :] = nothing
    blocks = blocks_of(per)
    for k, a in enumerate(range(0, DISP, STEP)):
        for i in range(0, len(blocks), 2):
            ours = [moved[k - 1, at] if k else anchor[at] for at in blocks[i : i + 2]]
            for b in range(min(STEP, DISP - a)):
                d = a + b
                tiles = []
                for m, at in zip(ours, blocks[i : i + 2]):
                    c = jnp.sum((m * (shifted[b - 1, at] if b else other[at])).reshape(per, 8, columns), axis=0)
                    c = along(c, a)
                    tiles.append(jnp.where(place >= d, c, 0.0) if d else c)
                high, low = split(jnp.concatenate(tiles, axis=0))
                at = slice((d + 1) * slab + i * 8, (d + 1) * slab + i * 8 + 16)
                c_high[at] = high
                c_low[at] = low


def filtered_pairs(half, banded, c_high, c_low):
    slab = 2 * GROUPS
    m = banded.shape[0] // 4
    weight = banded[pl.ds(pl.multiple_of(half * 2 * m, 2 * m), 2 * m)]
    for d in range(0, DISP, 2):
        at = [slice((d + k) * slab, (d + k + 3) * slab) for k in range(2)]
        high = jnp.concatenate([c_high[s] for s in at], axis=1)
        low = jnp.concatenate([c_low[s] for s in at], axis=1)
        y = mm(weight, high)
        yield d, y[:m] + (y[m:] + mm(weight[:m], low))


def near_kernel(flags, own, own_mate, partner, partner_mate, partner_far, conv_high, conv_low, lift_high, lift_low, banded, part, far_other, anchor, other, moved, shifted, c_high, c_low):
    half = 1 - flags[1]
    right = flags[0] == 1
    operands = (conv_high, conv_low, lift_high, lift_low)
    per = lift_high.shape[0] // GROUPS
    fours = [four_rows(half, own, own_mate), four_rows(half, partner, partner_mate)]
    features(fours, operands, [anchor, other], rows_inside(flags, half))
    move_anchor(right, anchor, moved, per)
    move_other(right, other, shifted, per)
    features([four_rows(1 - half, partner, partner_far)], operands, [far_other], rows_inside(flags, 1 - half))
    correlate(right, anchor, moved, other, shifted, c_high, c_low, per)
    for d, y in filtered_pairs(half, banded, c_high, c_low):
        part[d // 2] = y


def far_kernel(flags, own, own_far, other, conv_high, conv_low, lift_high, lift_low, banded, part, out, anchor, moved, shifted, c_high, c_low):
    half = flags[1]
    right = flags[0] == 1
    operands = (conv_high, conv_low, lift_high, lift_low)
    per = lift_high.shape[0] // GROUPS
    move_other(right, other, shifted, per)
    features([four_rows(half, own, own_far)], operands, [anchor], rows_inside(flags, half))
    move_anchor(right, anchor, moved, per)
    correlate(right, anchor, moved, other, shifted, c_high, c_low, per)
    columns = own.shape[2]
    outs = banded.shape[0] // 24
    for d, y in filtered_pairs(half, banded, c_high, c_low):
        y = y + part[d // 2]
        for k in range(2):
            for row in range(2):
                o = from_columns(y[row * 3 * outs : (row + 1) * 3 * outs, k * columns : (k + 1) * columns], outs)
                out[pl.ds(row * outs * DISP + d + k, outs, stride=DISP)] = o


def vmem():
    return pl.BlockSpec(memory_space=pltpu.VMEM)


def smem():
    return pl.BlockSpec(memory_space=pltpu.SMEM)


def call(kernel, name, out_shape, in_specs, scratch, *args):
    return pl.pallas_call(
        kernel,
        out_shape=out_shape,
        in_specs=in_specs,
        out_specs=jax.tree.map(lambda _: vmem(), out_shape),
        scratch_shapes=scratch,
        compiler_params=pltpu.CompilerParams(vmem_limit_bytes=VMEM_BYTES),
        cost_estimate=pl.CostEstimate(flops=COST, bytes_accessed=COST, transcendentals=0),
        name=name,
    )(*args)


def prepare(conv, lift, vol):
    channels = conv.shape[2]
    feats = lift.shape[0]
    shapes = [(3 * channels, 3 * channels)] * 2 + [(feats, channels)] * 2 + [(8 * 3 * vol.shape[3], 6 * GROUPS)]
    out = [jax.ShapeDtypeStruct(s, BF16) for s in shapes]
    scratch = [pltpu.VMEM(x.shape, F32) for x in (conv, lift, vol)] + [pltpu.SemaphoreType.DMA((3,))]
    args = [pltpu.with_memory_space_constraint(x, pltpu.HBM) for x in (conv, lift, vol)]
    return call(prepare_kernel, "prepare", out, [pl.BlockSpec(memory_space=pltpu.HBM)] * 3, scratch, *args)


def volume_scratch(feats, columns):
    depth = (DISP + 2) * 2 * GROUPS
    return [
        pltpu.VMEM((-(-DISP // STEP) - 1, 2 * feats, columns), F32),
        pltpu.VMEM((STEP - 1, 2 * feats, columns), F32),
        pltpu.VMEM((depth, columns), BF16),
        pltpu.VMEM((depth, columns), BF16),
    ]


def near(flags, own, own_mate, partner, partner_mate, partner_far, operands):
    columns = partner.shape[2]
    feats = operands[2].shape[0]
    out = [
        jax.ShapeDtypeStruct((DISP // 2, operands[4].shape[0] // 4, 2 * columns), F32),
        jax.ShapeDtypeStruct((2 * feats, columns), F32),
    ]
    scratch = [pltpu.VMEM((2 * feats, columns), F32)] * 2 + volume_scratch(feats, columns)
    args = (own, own_mate, partner, partner_mate, partner_far, *operands)
    return call(near_kernel, "near", out, [smem()] + [vmem()] * len(args), scratch, flags, *args)


def far(flags, own, own_far, other, operands, part):
    columns = own.shape[2]
    feats = operands[2].shape[0]
    out = jax.ShapeDtypeStruct((2 * operands[4].shape[0] // 24 * DISP, columns), F32)
    scratch = [pltpu.VMEM((2 * feats, columns), F32)] + volume_scratch(feats, columns)
    args = (own, own_far, other, *operands, part)
    return call(far_kernel, "far", out, [smem()] + [vmem()] * len(args), scratch, flags, *args)


def routes(size):
    half, quarter = size // 2, size // 4

    def across(i):
        return (i + 1) % size if i % 2 else (i - 1) % size

    def apart(i, j):
        low, high = min(i, j), max(i, j)
        return high - low == 1 and high in (quarter, 3 * quarter)

    every = range(size)
    swap = [(i, (i + half) % size) for i in every]
    mates = [(i, i ^ 1) for i in every if not apart(i, i ^ 1)]
    far = [(across(i), i) for i in every if not apart(i, across(i))]
    far_partner = [((i + half) % size, j) for i, j in far]
    return swap, mates, far, far_partner


def on_device(images, conv_weight, lift_weight, vol_weight):
    size = lax.axis_size("rows")
    position = lax.axis_index("rows")
    quarter = size // 4
    swap, mates, beyond, beyond_partner = routes(size)
    starts = (position == quarter) | (position == 3 * quarter)
    ends = (position == quarter - 1) | (position == 3 * quarter - 1)
    right = (position < quarter) | (position >= 3 * quarter)
    flags = jnp.stack([jnp.where(right, 1, 0), position % 2, jnp.where(starts, 0, 1), jnp.where(ends, 0, 1)]).astype(jnp.int32)

    partner = lax.ppermute(images, "rows", swap)
    partner_far = lax.ppermute(images, "rows", beyond_partner)
    own_mate = lax.ppermute(images, "rows", mates)
    own_far = lax.ppermute(images, "rows", beyond)
    partner_mate = lax.ppermute(partner, "rows", mates)
    operands = prepare(conv_weight, lift_weight, vol_weight)
    part, other = near(flags, images, own_mate, partner, partner_mate, partner_far, operands)
    whole = far(flags, images, own_far, other, operands, part)
    rows, _, columns = images.shape
    return whole.reshape(rows, vol_weight.shape[3], DISP, columns)


def solution(mesh):
    return jax.shard_map(
        on_device,
        mesh=mesh,
        in_specs=(P(("scenes", "rows"), None, None), P(), P(), P()),
        out_specs=P(("scenes", "rows"), None, None, None),
        check_vma=False,
    )
```

```python
import jax
import jax.numpy as jnp
from jax import lax
from jax.experimental import pallas as pl
from jax.experimental.pallas import tpu as pltpu
from jax.sharding import PartitionSpec as P

GROUPS = 40
DISP = 48
STEP = 8
CHUNK = 24
COST = 10**11
F32 = jnp.float32
BF16 = jnp.bfloat16
VMEM_BYTES = 24 * 1024 * 1024


def split(x):
    high = x.astype(BF16)
    return high, (x - high.astype(F32)).astype(BF16)


def mm(a, b):
    return jnp.dot(a, b, preferred_element_type=F32)


def from_columns(y, size):
    column = lax.broadcasted_iota(jnp.int32, (size, y.shape[1]), 1)
    last = y.shape[1] - 1
    left = jnp.where(column > 0, pltpu.roll(y[:size], 1, 1), 0.0)
    right = jnp.where(column < last, pltpu.roll(y[2 * size :], last, 1), 0.0)
    return y[size : 2 * size] + left + right


def stacked(high, low):
    return jnp.concatenate([high, high, low], axis=0)


def features(fours, conv, lift, tos, insides):
    channels = conv.shape[0] // 3
    columns = fours[0].shape[2]
    feats = lift.shape[0]
    at = [slice(k * channels, (k + 3) * channels) for k in range(2)]
    products = []
    for x in fours:
        parts = split(x.reshape(4 * channels, columns))
        products.append(mm(conv[...], stacked(*[jnp.concatenate([part[s] for s in at], axis=1) for part in parts])))
    halves = []
    for y, inside in zip(products, insides):
        hidden = []
        for k in range(2):
            h = jnp.maximum(from_columns(y[:, k * columns : (k + 1) * columns], channels), 0.0)
            hidden.append(jnp.where(inside[k], h, 0.0))
        halves.append(stacked(*split(jnp.concatenate(hidden, axis=1))))
    for h, to in zip(halves, tos):
        f = mm(lift[...], h)
        for k in range(2):
            to[k * feats : (k + 1) * feats] = f[:, k * columns : (k + 1) * columns]


def four_rows(half, block, beside):
    a, b = block[...], beside[...]
    first = half == 1
    return jnp.concatenate([jnp.where(first, a, b), jnp.where(first, b, a)], axis=0)


def rows_inside(flags, half):
    return [jnp.logical_or(half != k, flags[2 + k] == 1) for k in range(2)]


def prepare_kernel(conv_hbm, lift_hbm, vol_hbm, conv_out, lift_out, banded, conv, lift, vol, sems):
    pairs = ((conv_hbm, conv), (lift_hbm, lift), (vol_hbm, vol))
    copies = [pltpu.make_async_copy(a, b, sems.at[i]) for i, (a, b) in enumerate(pairs)]
    for copy in copies:
        copy.start()
    channels = conv.shape[2]
    depth = 3 * channels
    copies[0].wait()
    for dr in range(3):
        for dc in range(3):
            high, low = split(conv[dr, dc])
            for k, part in enumerate((high, low, high)):
                at = k * depth + dr * channels
                conv_out[dc * channels : (dc + 1) * channels, at : at + channels] = part
    feats = lift.shape[0]
    per = feats // GROUPS
    copies[1].wait()
    for g in range(0, feats, 8 * per):
        ordered = jnp.concatenate([lift[pl.ds(g + j, 8, stride=per)] for j in range(per)], axis=0)
        high, low = split(ordered)
        lift_out[g : g + 8 * per] = jnp.concatenate([high, low, high], axis=1)
    outs = vol.shape[3]
    m = 3 * outs
    nothing = jnp.zeros((m, GROUPS), F32)
    copies[2].wait()
    for half in range(2):
        for row in range(2):
            pieces = []
            for dd in range(3):
                for place in range(2):
                    dr = 2 * half + place - row
                    pieces.append(vol[dr, dd].reshape(m, GROUPS) * (1.0 / per) if 0 <= dr < 3 else nothing)
            high, low = split(jnp.concatenate(pieces, axis=1))
            banded[(4 * half + row) * m : (4 * half + row + 1) * m] = high
            banded[(4 * half + 2 + row) * m : (4 * half + 3 + row) * m] = low


def mover(right, columns):
    def along(x, d):
        if d == 0:
            return x
        there, back = d % columns, -d % columns
        return pltpu.roll(x, jnp.where(right, back, there), 1)

    return along


def blocks_of(per):
    block = 8 * per
    return [slice(i * block, (i + 1) * block) for i in range(2 * GROUPS // 8)]


def move_other(right, other, shifted, per):
    along = mover(right, other.shape[1])
    for at in blocks_of(per):
        values = other[at]
        for b in range(1, STEP):
            shifted[b - 1, at] = along(values, b)


def move_anchor(right, anchor, moved, per):
    along = mover(right, anchor.shape[1])
    for k, a in enumerate(range(STEP, DISP, STEP)):
        for at in blocks_of(per):
            moved[k, at] = along(anchor[at], -a)


def correlate(right, anchor, moved, other, shifted, c_high, c_low, per):
    columns = anchor.shape[1]
    along = mover(right, columns)
    column = lax.broadcasted_iota(jnp.int32, (8, columns), 1)
    place = jnp.where(right, columns - 1 - column, column)
    slab = 2 * GROUPS
    nothing = jnp.zeros((slab, columns), BF16)
    for c in (c_high, c_low):
        c[:slab] = nothing
        c[(DISP + 1) * slab :] = nothing
    blocks = blocks_of(per)
    for k, a in enumerate(range(0, DISP, STEP)):
        for i in range(0, len(blocks), 2):
            ours = [moved[k - 1, at] if k else anchor[at] for at in blocks[i : i + 2]]
            for b in range(min(STEP, DISP - a)):
                d = a + b
                tiles = []
                for m, at in zip(ours, blocks[i : i + 2]):
                    c = jnp.sum((m * (shifted[b - 1, at] if b else other[at])).reshape(per, 8, columns), axis=0)
                    c = along(c, a)
                    tiles.append(jnp.where(place >= d, c, 0.0) if d else c)
                high, low = split(jnp.concatenate(tiles, axis=0))
                at = slice((d + 1) * slab + i * 8, (d + 1) * slab + i * 8 + 16)
                c_high[at] = high
                c_low[at] = low


def filtered_pairs(half, banded, c_high, c_low):
    slab = 2 * GROUPS
    m = banded.shape[0] // 4
    weight = banded[pl.ds(pl.multiple_of(half * 2 * m, 2 * m), 2 * m)]
    for d in range(0, DISP, 2):
        at = [slice((d + k) * slab, (d + k + 3) * slab) for k in range(2)]
        high = jnp.concatenate([c_high[s] for s in at], axis=1)
        low = jnp.concatenate([c_low[s] for s in at], axis=1)
        y = mm(weight, high)
        yield d, y[:m] + (y[m:] + mm(weight[:m], low))


def near_kernel(flags, own, own_mate, partner, partner_mate, partner_far, conv, lift, banded, part, far_other, anchor, other, moved, shifted, c_high, c_low):
    half = 1 - flags[1]
    right = flags[0] == 1
    per = lift.shape[0] // GROUPS
    fours = [four_rows(half, own, own_mate), four_rows(half, partner, partner_mate), four_rows(1 - half, partner, partner_far)]
    insides = [rows_inside(flags, half)] * 2 + [rows_inside(flags, 1 - half)]
    features(fours, conv, lift, [anchor, other, far_other], insides)
    move_anchor(right, anchor, moved, per)
    move_other(right, other, shifted, per)
    correlate(right, anchor, moved, other, shifted, c_high, c_low, per)
    for d, y in filtered_pairs(half, banded, c_high, c_low):
        part[d // 2] = y


def far_kernel(flags, own, own_far, other, conv, lift, banded, part, result, anchor, moved, shifted, c_high, c_low, out, sems):
    half = flags[1]
    right = flags[0] == 1
    per = lift.shape[0] // GROUPS
    move_other(right, other, shifted, per)
    features([four_rows(half, own, own_far)], conv, lift, [anchor], [rows_inside(flags, half)])
    move_anchor(right, anchor, moved, per)
    correlate(right, anchor, moved, other, shifted, c_high, c_low, per)
    columns = own.shape[2]
    outs = banded.shape[0] // 24
    rows = 2 * outs
    copies = []
    for d, y in filtered_pairs(half, banded, c_high, c_low):
        y = y + part[d // 2]
        for k in range(2):
            for row in range(2):
                o = from_columns(y[row * 3 * outs : (row + 1) * 3 * outs, k * columns : (k + 1) * columns], outs)
                out[pl.ds(row * outs * DISP + d + k, outs, stride=DISP)] = o
        if (d + 2) % CHUNK == 0:
            i = d // CHUNK
            at = (slice(None), pl.ds(i * CHUNK, CHUNK))
            copies.append(pltpu.make_async_copy(out.reshape(rows, DISP, columns).at[at], result.at[at], sems.at[1 + i]))
            copies[-1].start()
    for copy in copies:
        copy.wait()


def vmem():
    return pl.BlockSpec(memory_space=pltpu.VMEM)


def smem():
    return pl.BlockSpec(memory_space=pltpu.SMEM)


def hbm():
    return pl.BlockSpec(memory_space=pltpu.HBM)


def call(kernel, name, out_shape, in_specs, scratch, *args, out_specs=None):
    return pl.pallas_call(
        kernel,
        out_shape=out_shape,
        in_specs=in_specs,
        out_specs=jax.tree.map(lambda _: vmem(), out_shape) if out_specs is None else out_specs,
        scratch_shapes=scratch,
        compiler_params=pltpu.CompilerParams(vmem_limit_bytes=VMEM_BYTES),
        cost_estimate=pl.CostEstimate(flops=COST, bytes_accessed=COST, transcendentals=0),
        name=name,
    )(*args)


def prepare(conv, lift, vol):
    channels = conv.shape[2]
    feats = lift.shape[0]
    shapes = [(3 * channels, 9 * channels), (feats, 3 * channels), (8 * 3 * vol.shape[3], 6 * GROUPS)]
    out = [jax.ShapeDtypeStruct(s, BF16) for s in shapes]
    scratch = [pltpu.VMEM(x.shape, F32) for x in (conv, lift, vol)] + [pltpu.SemaphoreType.DMA((3,))]
    args = [pltpu.with_memory_space_constraint(x, pltpu.HBM) for x in (conv, lift, vol)]
    return call(prepare_kernel, "prepare", out, [hbm()] * 3, scratch, *args)


def sizes(operands, columns):
    feats = operands[1].shape[0]
    plain = (2 * feats, columns)
    moved = (-(-DISP // STEP) - 1, 2 * feats, columns)
    shifted = (STEP - 1, 2 * feats, columns)
    volume = ((DISP + 2) * 2 * GROUPS, columns)
    part = (DISP // 2, operands[2].shape[0] // 4, 2 * columns)
    return plain, moved, shifted, volume, part


def near(flags, own, own_mate, partner, partner_mate, partner_far, operands):
    plain, moved, shifted, volume, part = sizes(operands, own.shape[2])
    scratch = [pltpu.VMEM(s, F32) for s in (plain, plain, moved, shifted)] + [pltpu.VMEM(volume, BF16)] * 2
    args = (own, own_mate, partner, partner_mate, partner_far, *operands)
    out = [jax.ShapeDtypeStruct(s, F32) for s in (part, plain)]
    return call(near_kernel, "near", out, [smem()] + [vmem()] * len(args), scratch, flags, *args)


def far(flags, own, own_far, other, operands, part):
    columns = own.shape[2]
    plain, moved, shifted, volume, _ = sizes(operands, columns)
    rows = operands[2].shape[0] // 12
    scratch = [pltpu.VMEM(s, F32) for s in (plain, moved, shifted)] + [pltpu.VMEM(volume, BF16)] * 2
    scratch += [pltpu.VMEM((rows * DISP, columns), F32), pltpu.SemaphoreType.DMA((1 + DISP // CHUNK,))]
    args = (own, own_far, other, *operands, part)
    in_specs = [smem()] + [vmem()] * len(args)
    out = jax.ShapeDtypeStruct((rows, DISP, columns), F32)
    return call(far_kernel, "far", out, in_specs, scratch, flags, *args, out_specs=hbm())


def routes(size):
    half, quarter = size // 2, size // 4

    def across(i):
        return (i + 1) % size if i % 2 else (i - 1) % size

    def apart(i, j):
        low, high = min(i, j), max(i, j)
        return high - low == 1 and high in (quarter, 3 * quarter)

    every = range(size)
    swap = [(i, (i + half) % size) for i in every]
    mates = [(i, i ^ 1) for i in every if not apart(i, i ^ 1)]
    far = [(across(i), i) for i in every if not apart(i, across(i))]
    far_partner = [((i + half) % size, j) for i, j in far]
    return swap, mates, far, far_partner


def on_device(images, conv_weight, lift_weight, vol_weight):
    size = lax.axis_size("rows")
    position = lax.axis_index("rows")
    quarter = size // 4
    swap, mates, beyond, beyond_partner = routes(size)
    starts = (position == quarter) | (position == 3 * quarter)
    ends = (position == quarter - 1) | (position == 3 * quarter - 1)
    right = (position < quarter) | (position >= 3 * quarter)
    flags = jnp.stack([jnp.where(right, 1, 0), position % 2, jnp.where(starts, 0, 1), jnp.where(ends, 0, 1)]).astype(jnp.int32)

    partner = lax.ppermute(images, "rows", swap)
    partner_far = lax.ppermute(images, "rows", beyond_partner)
    own_mate = lax.ppermute(images, "rows", mates)
    own_far = lax.ppermute(images, "rows", beyond)
    partner_mate = lax.ppermute(partner, "rows", mates)
    operands = prepare(conv_weight, lift_weight, vol_weight)
    part, other = near(flags, images, own_mate, partner, partner_mate, partner_far, operands)
    whole = far(flags, images, own_far, other, operands, part)
    rows, _, columns = images.shape
    return whole.reshape(rows, vol_weight.shape[3], DISP, columns)


def solution(mesh):
    return jax.shard_map(
        on_device,
        mesh=mesh,
        in_specs=(P(("scenes", "rows"), None, None), P(), P(), P()),
        out_specs=P(("scenes", "rows"), None, None, None),
        check_vma=False,
    )
```

```python
import jax
import jax.numpy as jnp
from jax import lax
from jax.experimental import pallas as pl
from jax.experimental.pallas import tpu as pltpu
from jax.sharding import PartitionSpec as P

GROUPS = 40
DISP = 48
STEP = 8
CHUNK = 24
COST = 10**10
BYTES = 10**7
F32 = jnp.float32
BF16 = jnp.bfloat16
VMEM_BYTES = 24 * 1024 * 1024


def split(x):
    high = x.astype(BF16)
    return high, (x - high.astype(F32)).astype(BF16)


def mm(a, b):
    return jnp.dot(a, b, preferred_element_type=F32)


def from_columns(y, size):
    column = lax.broadcasted_iota(jnp.int32, (size, y.shape[1]), 1)
    last = y.shape[1] - 1
    left = jnp.where(column > 0, pltpu.roll(y[:size], 1, 1), 0.0)
    right = jnp.where(column < last, pltpu.roll(y[2 * size :], last, 1), 0.0)
    return y[size : 2 * size] + left + right


def stacked(high, low):
    return jnp.concatenate([high, high, low], axis=0)


def features(fours, conv, lift, tos, insides):
    channels = conv.shape[0] // 3
    columns = fours[0].shape[2]
    feats = lift.shape[0]
    at = [slice(k * channels, (k + 3) * channels) for k in range(2)]
    products = []
    for x in fours:
        parts = split(x.reshape(4 * channels, columns))
        products.append(mm(conv[...], stacked(*[jnp.concatenate([part[s] for s in at], axis=1) for part in parts])))
    halves = []
    for y, inside in zip(products, insides):
        hidden = []
        for k in range(2):
            h = jnp.maximum(from_columns(y[:, k * columns : (k + 1) * columns], channels), 0.0)
            hidden.append(jnp.where(inside[k], h, 0.0))
        halves.append(stacked(*split(jnp.concatenate(hidden, axis=1))))
    for h, to in zip(halves, tos):
        f = mm(lift[...], h)
        for k in range(2):
            to[k * feats : (k + 1) * feats] = f[:, k * columns : (k + 1) * columns]


def four_rows(half, block, beside):
    a, b = block[...], beside[...]
    first = half == 1
    return jnp.concatenate([jnp.where(first, a, b), jnp.where(first, b, a)], axis=0)


def rows_inside(flags, half):
    return [jnp.logical_or(half != k, flags[2 + k] == 1) for k in range(2)]


def prepare_kernel(conv_hbm, lift_hbm, vol_hbm, mate, conv_out, lift_out, banded, conv, lift, vol, sems):
    pairs = ((conv_hbm, conv), (lift_hbm, lift), (vol_hbm, vol))
    copies = [pltpu.make_async_copy(a, b, sems.at[i]) for i, (a, b) in enumerate(pairs)]
    for copy in copies:
        copy.start()
    channels = conv.shape[2]
    depth = 3 * channels
    copies[0].wait()
    for dr in range(3):
        for dc in range(3):
            high, low = split(conv[dr, dc])
            for k, part in enumerate((high, low, high)):
                at = k * depth + dr * channels
                conv_out[dc * channels : (dc + 1) * channels, at : at + channels] = part
    feats = lift.shape[0]
    per = feats // GROUPS
    copies[1].wait()
    for g in range(0, feats, 8 * per):
        ordered = jnp.concatenate([lift[pl.ds(g + j, 8, stride=per)] for j in range(per)], axis=0)
        high, low = split(ordered)
        lift_out[g : g + 8 * per] = jnp.concatenate([high, low, high], axis=1)
    outs = vol.shape[3]
    m = 3 * outs
    nothing = jnp.zeros((m, GROUPS), F32)
    copies[2].wait()
    for half in range(2):
        for row in range(2):
            pieces = []
            for dd in range(3):
                for place in range(2):
                    dr = 2 * half + place - row
                    pieces.append(vol[dr, dd].reshape(m, GROUPS) * (1.0 / per) if 0 <= dr < 3 else nothing)
            high, low = split(jnp.concatenate(pieces, axis=1))
            banded[(4 * half + row) * m : (4 * half + row + 1) * m] = high
            banded[(4 * half + 2 + row) * m : (4 * half + 3 + row) * m] = low


def mover(right, columns):
    def along(x, d):
        if d == 0:
            return x
        there, back = d % columns, -d % columns
        return pltpu.roll(x, jnp.where(right, back, there), 1)

    return along


def blocks_of(per):
    block = 8 * per
    return [slice(i * block, (i + 1) * block) for i in range(2 * GROUPS // 8)]


def move_other(right, other, shifted, per):
    along = mover(right, other.shape[1])
    for at in blocks_of(per):
        values = other[at]
        for b in range(1, STEP):
            shifted[b - 1, at] = along(values, b)


def move_anchor(right, anchor, moved, per):
    along = mover(right, anchor.shape[1])
    for k, a in enumerate(range(STEP, DISP, STEP)):
        for at in blocks_of(per):
            moved[k, at] = along(anchor[at], -a)


def correlate(right, anchor, moved, other, shifted, c_high, c_low, per):
    columns = anchor.shape[1]
    along = mover(right, columns)
    column = lax.broadcasted_iota(jnp.int32, (8, columns), 1)
    place = jnp.where(right, columns - 1 - column, column)
    slab = 2 * GROUPS
    nothing = jnp.zeros((slab, columns), BF16)
    for c in (c_high, c_low):
        c[:slab] = nothing
        c[(DISP + 1) * slab :] = nothing
    blocks = blocks_of(per)
    for k, a in enumerate(range(0, DISP, STEP)):
        for i in range(0, len(blocks), 2):
            ours = [moved[k - 1, at] if k else anchor[at] for at in blocks[i : i + 2]]
            for b in range(min(STEP, DISP - a)):
                d = a + b
                tiles = []
                for m, at in zip(ours, blocks[i : i + 2]):
                    c = jnp.sum((m * (shifted[b - 1, at] if b else other[at])).reshape(per, 8, columns), axis=0)
                    c = along(c, a)
                    tiles.append(jnp.where(place >= d, c, 0.0) if d else c)
                high, low = split(jnp.concatenate(tiles, axis=0))
                at = slice((d + 1) * slab + i * 8, (d + 1) * slab + i * 8 + 16)
                c_high[at] = high
                c_low[at] = low


def filtered_pairs(half, banded, c_high, c_low):
    slab = 2 * GROUPS
    m = banded.shape[0] // 4
    weight = banded[pl.ds(pl.multiple_of(half * 2 * m, 2 * m), 2 * m)]
    for d in range(0, DISP, 2):
        at = [slice((d + k) * slab, (d + k + 3) * slab) for k in range(2)]
        high = jnp.concatenate([c_high[s] for s in at], axis=1)
        low = jnp.concatenate([c_low[s] for s in at], axis=1)
        y = mm(weight, high)
        yield d, y[:m] + (y[m:] + mm(weight[:m], low))


def near_kernel(flags, own, own_mate, partner, partner_mate, conv, lift, banded, part, anchor, other, moved, shifted, c_high, c_low):
    half = 1 - flags[1]
    right = flags[0] == 1
    per = lift.shape[0] // GROUPS
    fours = [four_rows(half, own, own_mate), four_rows(half, partner, partner_mate)]
    features(fours, conv, lift, [anchor, other], [rows_inside(flags, half)] * 2)
    move_anchor(right, anchor, moved, per)
    move_other(right, other, shifted, per)
    correlate(right, anchor, moved, other, shifted, c_high, c_low, per)
    for d, y in filtered_pairs(half, banded, c_high, c_low):
        part[d // 2] = y


def far_kernel(flags, own, own_far, partner, partner_far, conv, lift, banded, part, result, anchor, other, moved, shifted, c_high, c_low, out, sems):
    half = flags[1]
    right = flags[0] == 1
    per = lift.shape[0] // GROUPS
    fours = [four_rows(half, own, own_far), four_rows(half, partner, partner_far)]
    features(fours, conv, lift, [anchor, other], [rows_inside(flags, half)] * 2)
    move_other(right, other, shifted, per)
    move_anchor(right, anchor, moved, per)
    correlate(right, anchor, moved, other, shifted, c_high, c_low, per)
    columns = own.shape[2]
    outs = banded.shape[0] // 24
    rows = 2 * outs
    copies = []
    for d, y in filtered_pairs(half, banded, c_high, c_low):
        y = y + part[d // 2]
        for k in range(2):
            for row in range(2):
                o = from_columns(y[row * 3 * outs : (row + 1) * 3 * outs, k * columns : (k + 1) * columns], outs)
                out[pl.ds(row * outs * DISP + d + k, outs, stride=DISP)] = o
        if (d + 2) % CHUNK == 0:
            i = d // CHUNK
            at = (slice(None), pl.ds(i * CHUNK, CHUNK))
            copies.append(pltpu.make_async_copy(out.reshape(rows, DISP, columns).at[at], result.at[at], sems.at[1 + i]))
            copies[-1].start()
    for copy in copies:
        copy.wait()


def vmem():
    return pl.BlockSpec(memory_space=pltpu.VMEM)


def smem():
    return pl.BlockSpec(memory_space=pltpu.SMEM)


def hbm():
    return pl.BlockSpec(memory_space=pltpu.HBM)


def call(kernel, name, out_shape, in_specs, scratch, *args, out_specs=None):
    return pl.pallas_call(
        kernel,
        out_shape=out_shape,
        in_specs=in_specs,
        out_specs=jax.tree.map(lambda _: vmem(), out_shape) if out_specs is None else out_specs,
        scratch_shapes=scratch,
        compiler_params=pltpu.CompilerParams(vmem_limit_bytes=VMEM_BYTES),
        cost_estimate=pl.CostEstimate(flops=COST, bytes_accessed=BYTES, transcendentals=0),
        name=name,
    )(*args)


def prepare(conv, lift, vol, mate):
    channels = conv.shape[2]
    feats = lift.shape[0]
    shapes = [(3 * channels, 9 * channels), (feats, 3 * channels), (8 * 3 * vol.shape[3], 6 * GROUPS)]
    out = [jax.ShapeDtypeStruct(s, BF16) for s in shapes]
    scratch = [pltpu.VMEM(x.shape, F32) for x in (conv, lift, vol)] + [pltpu.SemaphoreType.DMA((3,))]
    args = [pltpu.with_memory_space_constraint(x, pltpu.HBM) for x in (conv, lift, vol)]
    return call(prepare_kernel, "prepare", out, [hbm()] * 3 + [pl.BlockSpec(memory_space=pl.ANY)], scratch, *args, mate)


def sizes(operands, columns):
    feats = operands[1].shape[0]
    plain = (2 * feats, columns)
    moved = (-(-DISP // STEP) - 1, 2 * feats, columns)
    shifted = (STEP - 1, 2 * feats, columns)
    volume = ((DISP + 2) * 2 * GROUPS, columns)
    part = (DISP // 2, operands[2].shape[0] // 4, 2 * columns)
    return plain, moved, shifted, volume, part


def near(flags, own, own_mate, partner, partner_mate, operands):
    plain, moved, shifted, volume, part = sizes(operands, own.shape[2])
    scratch = [pltpu.VMEM(s, F32) for s in (plain, plain, moved, shifted)] + [pltpu.VMEM(volume, BF16)] * 2
    args = (own, own_mate, partner, partner_mate, *operands)
    out = jax.ShapeDtypeStruct(part, F32)
    return call(near_kernel, "near", out, [smem()] + [vmem()] * len(args), scratch, flags, *args)


def far(flags, own, own_far, partner, partner_far, operands, part):
    columns = own.shape[2]
    plain, moved, shifted, volume, _ = sizes(operands, columns)
    rows = operands[2].shape[0] // 12
    scratch = [pltpu.VMEM(s, F32) for s in (plain, plain, moved, shifted)] + [pltpu.VMEM(volume, BF16)] * 2
    scratch += [pltpu.VMEM((rows * DISP, columns), F32), pltpu.SemaphoreType.DMA((1 + DISP // CHUNK,))]
    args = (own, own_far, partner, partner_far, *operands, part)
    in_specs = [smem()] + [vmem()] * len(args)
    out = jax.ShapeDtypeStruct((rows, DISP, columns), F32)
    return call(far_kernel, "far", out, in_specs, scratch, flags, *args, out_specs=hbm())


def routes(size):
    half, quarter = size // 2, size // 4

    def across(i):
        return (i + 1) % size if i % 2 else (i - 1) % size

    def apart(i, j):
        low, high = min(i, j), max(i, j)
        return high - low == 1 and high in (quarter, 3 * quarter)

    every = range(size)
    swap = [(i, (i + half) % size) for i in every]
    mates = [(i, i ^ 1) for i in every if not apart(i, i ^ 1)]
    far = [(across(i), i) for i in every if not apart(i, across(i))]
    far_partner = [((i + half) % size, j) for i, j in far]
    return swap, mates, far, far_partner


def on_device(images, conv_weight, lift_weight, vol_weight):
    size = lax.axis_size("rows")
    position = lax.axis_index("rows")
    quarter = size // 4
    swap, mates, beyond, beyond_partner = routes(size)
    starts = (position == quarter) | (position == 3 * quarter)
    ends = (position == quarter - 1) | (position == 3 * quarter - 1)
    right = (position < quarter) | (position >= 3 * quarter)
    flags = jnp.stack([jnp.where(right, 1, 0), position % 2, jnp.where(starts, 0, 1), jnp.where(ends, 0, 1)]).astype(jnp.int32)

    partner = lax.ppermute(images, "rows", swap)
    partner_far = lax.ppermute(images, "rows", beyond_partner)
    own_mate = lax.ppermute(images, "rows", mates)
    own_far = lax.ppermute(images, "rows", beyond)
    partner_mate = lax.ppermute(partner, "rows", mates)
    operands = prepare(conv_weight, lift_weight, vol_weight, own_mate)
    part = near(flags, images, own_mate, partner, partner_mate, operands)
    whole = far(flags, images, own_far, partner, partner_far, operands, part)
    rows, _, columns = images.shape
    return whole.reshape(rows, vol_weight.shape[3], DISP, columns)


def solution(mesh):
    return jax.shard_map(
        on_device,
        mesh=mesh,
        in_specs=(P(("scenes", "rows"), None, None), P(), P(), P()),
        out_specs=P(("scenes", "rows"), None, None, None),
        check_vma=False,
    )
```

```python
import jax
import jax.numpy as jnp
from jax import lax
from jax.experimental import pallas as pl
from jax.experimental.pallas import tpu as pltpu
from jax.sharding import PartitionSpec as P

GROUPS = 40
DISP = 48
STEP = 8
CHUNK = 16
COST = 10**10
BYTES = 10**7
F32 = jnp.float32
BF16 = jnp.bfloat16
VMEM_BYTES = 24 * 1024 * 1024


def split(x):
    high = x.astype(BF16)
    return high, (x - high.astype(F32)).astype(BF16)


def mm(a, b):
    return jnp.dot(a, b, preferred_element_type=F32)


def from_columns(y, size):
    column = lax.broadcasted_iota(jnp.int32, (size, y.shape[1]), 1)
    last = y.shape[1] - 1
    left = jnp.where(column > 0, pltpu.roll(y[:size], 1, 1), 0.0)
    right = jnp.where(column < last, pltpu.roll(y[2 * size :], last, 1), 0.0)
    return y[size : 2 * size] + left + right


def stacked(high, low):
    return jnp.concatenate([high, high, low], axis=0)


def features(fours, conv, lift, tos, insides):
    channels = conv.shape[0] // 3
    columns = fours[0].shape[2]
    feats = lift.shape[0]
    at = [slice(k * channels, (k + 3) * channels) for k in range(2)]
    products = []
    for x in fours:
        parts = split(x.reshape(4 * channels, columns))
        products.append(mm(conv[...], stacked(*[jnp.concatenate([part[s] for s in at], axis=1) for part in parts])))
    halves = []
    for y, inside in zip(products, insides):
        hidden = []
        for k in range(2):
            h = jnp.maximum(from_columns(y[:, k * columns : (k + 1) * columns], channels), 0.0)
            hidden.append(jnp.where(inside[k], h, 0.0))
        halves.append(stacked(*split(jnp.concatenate(hidden, axis=1))))
    for h, to in zip(halves, tos):
        f = mm(lift[...], h)
        for k in range(2):
            to[k * feats : (k + 1) * feats] = f[:, k * columns : (k + 1) * columns]


def four_rows(half, block, beside):
    a, b = block[...], beside[...]
    first = half == 1
    return jnp.concatenate([jnp.where(first, a, b), jnp.where(first, b, a)], axis=0)


def rows_inside(flags, half):
    return [jnp.logical_or(half != k, flags[2 + k] == 1) for k in range(2)]


def prepare_kernel(conv_hbm, lift_hbm, vol_hbm, mate, conv_out, lift_out, banded, conv, lift, vol, sems):
    pairs = ((conv_hbm, conv), (lift_hbm, lift), (vol_hbm, vol))
    copies = [pltpu.make_async_copy(a, b, sems.at[i]) for i, (a, b) in enumerate(pairs)]
    for copy in copies:
        copy.start()
    channels = conv.shape[2]
    depth = 3 * channels
    copies[0].wait()
    for dr in range(3):
        for dc in range(3):
            high, low = split(conv[dr, dc])
            for k, part in enumerate((high, low, high)):
                at = k * depth + dr * channels
                conv_out[dc * channels : (dc + 1) * channels, at : at + channels] = part
    feats = lift.shape[0]
    per = feats // GROUPS
    copies[1].wait()
    for g in range(0, feats, 8 * per):
        ordered = jnp.concatenate([lift[pl.ds(g + j, 8, stride=per)] for j in range(per)], axis=0)
        high, low = split(ordered)
        lift_out[g : g + 8 * per] = jnp.concatenate([high, low, high], axis=1)
    outs = vol.shape[3]
    m = 3 * outs
    nothing = jnp.zeros((m, GROUPS), F32)
    copies[2].wait()
    for half in range(2):
        for row in range(2):
            pieces = []
            for dd in range(3):
                for place in range(2):
                    dr = 2 * half + place - row
                    pieces.append(vol[dr, dd].reshape(m, GROUPS) * (1.0 / per) if 0 <= dr < 3 else nothing)
            high, low = split(jnp.concatenate(pieces, axis=1))
            banded[(4 * half + row) * m : (4 * half + row + 1) * m] = high
            banded[(4 * half + 2 + row) * m : (4 * half + 3 + row) * m] = low


def mover(right, columns):
    def along(x, d):
        if d == 0:
            return x
        there, back = d % columns, -d % columns
        return pltpu.roll(x, jnp.where(right, back, there), 1)

    return along


def blocks_of(per):
    block = 8 * per
    return [slice(i * block, (i + 1) * block) for i in range(2 * GROUPS // 8)]


def move_other(right, other, shifted, per):
    along = mover(right, other.shape[1])
    for at in blocks_of(per):
        values = other[at]
        for b in range(1, STEP):
            shifted[b - 1, at] = along(values, b)


def move_anchor(right, anchor, moved, per):
    along = mover(right, anchor.shape[1])
    for k, a in enumerate(range(STEP, DISP, STEP)):
        for at in blocks_of(per):
            moved[k, at] = along(anchor[at], -a)


def correlate(right, anchor, moved, other, shifted, c_high, c_low, per):
    columns = anchor.shape[1]
    along = mover(right, columns)
    column = lax.broadcasted_iota(jnp.int32, (8, columns), 1)
    place = jnp.where(right, columns - 1 - column, column)
    slab = 2 * GROUPS
    nothing = jnp.zeros((slab, columns), BF16)
    for c in (c_high, c_low):
        c[:slab] = nothing
        c[(DISP + 1) * slab :] = nothing
    blocks = blocks_of(per)
    for k, a in enumerate(range(0, DISP, STEP)):
        for i in range(0, len(blocks), 2):
            ours = [moved[k - 1, at] if k else anchor[at] for at in blocks[i : i + 2]]
            for b in range(min(STEP, DISP - a)):
                d = a + b
                tiles = []
                for m, at in zip(ours, blocks[i : i + 2]):
                    c = jnp.sum((m * (shifted[b - 1, at] if b else other[at])).reshape(per, 8, columns), axis=0)
                    c = along(c, a)
                    tiles.append(jnp.where(place >= d, c, 0.0) if d else c)
                high, low = split(jnp.concatenate(tiles, axis=0))
                at = slice((d + 1) * slab + i * 8, (d + 1) * slab + i * 8 + 16)
                c_high[at] = high
                c_low[at] = low


def filtered_pairs(half, banded, c_high, c_low):
    slab = 2 * GROUPS
    m = banded.shape[0] // 4
    weight = banded[pl.ds(pl.multiple_of(half * 2 * m, 2 * m), 2 * m)]
    for d in range(0, DISP, 2):
        at = [slice((d + k) * slab, (d + k + 3) * slab) for k in range(2)]
        high = jnp.concatenate([c_high[s] for s in at], axis=1)
        low = jnp.concatenate([c_low[s] for s in at], axis=1)
        y = mm(weight, high)
        yield d, y[:m] + (y[m:] + mm(weight[:m], low))


def near_kernel(flags, own, own_mate, partner, partner_mate, conv, lift, banded, part, anchor, other, moved, shifted, c_high, c_low):
    half = 1 - flags[1]
    right = flags[0] == 1
    per = lift.shape[0] // GROUPS
    fours = [four_rows(half, own, own_mate), four_rows(half, partner, partner_mate)]
    features(fours, conv, lift, [anchor, other], [rows_inside(flags, half)] * 2)
    move_anchor(right, anchor, moved, per)
    move_other(right, other, shifted, per)
    correlate(right, anchor, moved, other, shifted, c_high, c_low, per)
    for d, y in filtered_pairs(half, banded, c_high, c_low):
        part[d // 2] = y


def far_kernel(flags, own, own_far, partner, partner_far, conv, lift, banded, part, result, anchor, other, moved, shifted, c_high, c_low, out, sems):
    half = flags[1]
    right = flags[0] == 1
    per = lift.shape[0] // GROUPS
    fours = [four_rows(half, own, own_far), four_rows(half, partner, partner_far)]
    features(fours, conv, lift, [anchor, other], [rows_inside(flags, half)] * 2)
    move_other(right, other, shifted, per)
    move_anchor(right, anchor, moved, per)
    correlate(right, anchor, moved, other, shifted, c_high, c_low, per)
    columns = own.shape[2]
    outs = banded.shape[0] // 24
    rows = 2 * outs
    copies = []
    for d, y in filtered_pairs(half, banded, c_high, c_low):
        y = y + part[d // 2]
        for k in range(2):
            for row in range(2):
                o = from_columns(y[row * 3 * outs : (row + 1) * 3 * outs, k * columns : (k + 1) * columns], outs)
                out[pl.ds(row * outs * DISP + d + k, outs, stride=DISP)] = o
        if (d + 2) % CHUNK == 0:
            i = d // CHUNK
            at = (slice(None), pl.ds(i * CHUNK, CHUNK))
            copies.append(pltpu.make_async_copy(out.reshape(rows, DISP, columns).at[at], result.at[at], sems.at[1 + i]))
            copies[-1].start()
    for copy in copies:
        copy.wait()


def vmem():
    return pl.BlockSpec(memory_space=pltpu.VMEM)


def smem():
    return pl.BlockSpec(memory_space=pltpu.SMEM)


def hbm():
    return pl.BlockSpec(memory_space=pltpu.HBM)


def call(kernel, name, out_shape, in_specs, scratch, *args, out_specs=None):
    return pl.pallas_call(
        kernel,
        out_shape=out_shape,
        in_specs=in_specs,
        out_specs=jax.tree.map(lambda _: vmem(), out_shape) if out_specs is None else out_specs,
        scratch_shapes=scratch,
        compiler_params=pltpu.CompilerParams(vmem_limit_bytes=VMEM_BYTES),
        cost_estimate=pl.CostEstimate(flops=COST, bytes_accessed=BYTES, transcendentals=0),
        name=name,
    )(*args)


def prepare(conv, lift, vol, mate):
    channels = conv.shape[2]
    feats = lift.shape[0]
    shapes = [(3 * channels, 9 * channels), (feats, 3 * channels), (8 * 3 * vol.shape[3], 6 * GROUPS)]
    out = [jax.ShapeDtypeStruct(s, BF16) for s in shapes]
    scratch = [pltpu.VMEM(x.shape, F32) for x in (conv, lift, vol)] + [pltpu.SemaphoreType.DMA((3,))]
    args = [pltpu.with_memory_space_constraint(x, pltpu.HBM) for x in (conv, lift, vol)]
    return call(prepare_kernel, "prepare", out, [hbm()] * 3 + [pl.BlockSpec(memory_space=pl.ANY)], scratch, *args, mate)


def sizes(operands, columns):
    feats = operands[1].shape[0]
    plain = (2 * feats, columns)
    moved = (-(-DISP // STEP) - 1, 2 * feats, columns)
    shifted = (STEP - 1, 2 * feats, columns)
    volume = ((DISP + 2) * 2 * GROUPS, columns)
    part = (DISP // 2, operands[2].shape[0] // 4, 2 * columns)
    return plain, moved, shifted, volume, part


def near(flags, own, own_mate, partner, partner_mate, operands):
    plain, moved, shifted, volume, part = sizes(operands, own.shape[2])
    scratch = [pltpu.VMEM(s, F32) for s in (plain, plain, moved, shifted)] + [pltpu.VMEM(volume, BF16)] * 2
    args = (own, own_mate, partner, partner_mate, *operands)
    out = jax.ShapeDtypeStruct(part, F32)
    return call(near_kernel, "near", out, [smem()] + [vmem()] * len(args), scratch, flags, *args)


def far(flags, own, own_far, partner, partner_far, operands, part):
    columns = own.shape[2]
    plain, moved, shifted, volume, _ = sizes(operands, columns)
    rows = operands[2].shape[0] // 12
    scratch = [pltpu.VMEM(s, F32) for s in (plain, plain, moved, shifted)] + [pltpu.VMEM(volume, BF16)] * 2
    scratch += [pltpu.VMEM((rows * DISP, columns), F32), pltpu.SemaphoreType.DMA((1 + DISP // CHUNK,))]
    args = (own, own_far, partner, partner_far, *operands, part)
    in_specs = [smem()] + [vmem()] * len(args)
    out = jax.ShapeDtypeStruct((rows, DISP, columns), F32)
    return call(far_kernel, "far", out, in_specs, scratch, flags, *args, out_specs=hbm())


def routes(size):
    half, quarter = size // 2, size // 4

    def across(i):
        return (i + 1) % size if i % 2 else (i - 1) % size

    def apart(i, j):
        low, high = min(i, j), max(i, j)
        return high - low == 1 and high in (quarter, 3 * quarter)

    every = range(size)
    swap = [(i, (i + half) % size) for i in every]
    mates = [(i, i ^ 1) for i in every if not apart(i, i ^ 1)]
    far = [(across(i), i) for i in every if not apart(i, across(i))]
    far_partner = [((i + half) % size, j) for i, j in far]
    return swap, mates, far, far_partner


def on_device(images, conv_weight, lift_weight, vol_weight):
    size = lax.axis_size("rows")
    position = lax.axis_index("rows")
    quarter = size // 4
    swap, mates, beyond, beyond_partner = routes(size)
    starts = (position == quarter) | (position == 3 * quarter)
    ends = (position == quarter - 1) | (position == 3 * quarter - 1)
    right = (position < quarter) | (position >= 3 * quarter)
    flags = jnp.stack([jnp.where(right, 1, 0), position % 2, jnp.where(starts, 0, 1), jnp.where(ends, 0, 1)]).astype(jnp.int32)

    partner = lax.ppermute(images, "rows", swap)
    partner_far = lax.ppermute(images, "rows", beyond_partner)
    own_mate = lax.ppermute(images, "rows", mates)
    own_far = lax.ppermute(images, "rows", beyond)
    partner_mate = lax.ppermute(partner, "rows", mates)
    operands = prepare(conv_weight, lift_weight, vol_weight, own_mate)
    part = near(flags, images, own_mate, partner, partner_mate, operands)
    whole = far(flags, images, own_far, partner, partner_far, operands, part)
    rows, _, columns = images.shape
    return whole.reshape(rows, vol_weight.shape[3], DISP, columns)


def solution(mesh):
    return jax.shard_map(
        on_device,
        mesh=mesh,
        in_specs=(P(("scenes", "rows"), None, None), P(), P(), P()),
        out_specs=P(("scenes", "rows"), None, None, None),
        check_vma=False,
    )
```

```python
import jax
import jax.numpy as jnp
from jax import lax
from jax.experimental import pallas as pl
from jax.experimental.pallas import tpu as pltpu
from jax.sharding import PartitionSpec as P

GROUPS = 40
DISP = 48
STEP = 8
LAST = 8
COST = 10**10
BYTES = 10**7
F32 = jnp.float32
BF16 = jnp.bfloat16
VMEM_BYTES = 24 * 1024 * 1024


def split(x):
    high = x.astype(BF16)
    return high, (x - high.astype(F32)).astype(BF16)


def mm(a, b):
    return jnp.dot(a, b, preferred_element_type=F32)


def from_columns(y, size):
    column = lax.broadcasted_iota(jnp.int32, (size, y.shape[1]), 1)
    last = y.shape[1] - 1
    left = jnp.where(column > 0, pltpu.roll(y[:size], 1, 1), 0.0)
    right = jnp.where(column < last, pltpu.roll(y[2 * size :], last, 1), 0.0)
    return y[size : 2 * size] + left + right


def stacked(high, low):
    return jnp.concatenate([high, high, low], axis=0)


def features(fours, conv, lift, tos, insides):
    channels = conv.shape[0] // 3
    columns = fours[0].shape[2]
    feats = lift.shape[0]
    at = [slice(k * channels, (k + 3) * channels) for k in range(2)]
    products = []
    for x in fours:
        parts = split(x.reshape(4 * channels, columns))
        products.append(mm(conv[...], stacked(*[jnp.concatenate([part[s] for s in at], axis=1) for part in parts])))
    halves = []
    for y, inside in zip(products, insides):
        hidden = []
        for k in range(2):
            h = jnp.maximum(from_columns(y[:, k * columns : (k + 1) * columns], channels), 0.0)
            hidden.append(jnp.where(inside[k], h, 0.0))
        halves.append(stacked(*split(jnp.concatenate(hidden, axis=1))))
    for h, to in zip(halves, tos):
        f = mm(lift[...], h)
        for k in range(2):
            to[k * feats : (k + 1) * feats] = f[:, k * columns : (k + 1) * columns]


def four_rows(half, block, beside):
    a, b = block[...], beside[...]
    first = half == 1
    return jnp.concatenate([jnp.where(first, a, b), jnp.where(first, b, a)], axis=0)


def rows_inside(flags, half):
    return [jnp.logical_or(half != k, flags[2 + k] == 1) for k in range(2)]


def prepare_kernel(conv_hbm, lift_hbm, vol_hbm, mate, conv_out, lift_out, banded, conv, lift, vol, sems):
    pairs = ((conv_hbm, conv), (lift_hbm, lift), (vol_hbm, vol))
    copies = [pltpu.make_async_copy(a, b, sems.at[i]) for i, (a, b) in enumerate(pairs)]
    for copy in copies:
        copy.start()
    channels = conv.shape[2]
    depth = 3 * channels
    copies[0].wait()
    for dr in range(3):
        for dc in range(3):
            high, low = split(conv[dr, dc])
            for k, part in enumerate((high, low, high)):
                at = k * depth + dr * channels
                conv_out[dc * channels : (dc + 1) * channels, at : at + channels] = part
    feats = lift.shape[0]
    per = feats // GROUPS
    copies[1].wait()
    for g in range(0, feats, 8 * per):
        ordered = jnp.concatenate([lift[pl.ds(g + j, 8, stride=per)] for j in range(per)], axis=0)
        high, low = split(ordered)
        lift_out[g : g + 8 * per] = jnp.concatenate([high, low, high], axis=1)
    outs = vol.shape[3]
    m = 3 * outs
    nothing = jnp.zeros((m, GROUPS), F32)
    copies[2].wait()
    for half in range(2):
        for row in range(2):
            pieces = []
            for dd in range(3):
                for place in range(2):
                    dr = 2 * half + place - row
                    pieces.append(vol[dr, dd].reshape(m, GROUPS) * (1.0 / per) if 0 <= dr < 3 else nothing)
            high, low = split(jnp.concatenate(pieces, axis=1))
            banded[(4 * half + row) * m : (4 * half + row + 1) * m] = high
            banded[(4 * half + 2 + row) * m : (4 * half + 3 + row) * m] = low


def mover(right, columns):
    def along(x, d):
        if d == 0:
            return x
        there, back = d % columns, -d % columns
        return pltpu.roll(x, jnp.where(right, back, there), 1)

    return along


def blocks_of(per):
    block = 8 * per
    return [slice(i * block, (i + 1) * block) for i in range(2 * GROUPS // 8)]


def move_other(right, other, shifted, per):
    along = mover(right, other.shape[1])
    for at in blocks_of(per):
        values = other[at]
        for b in range(1, STEP):
            shifted[b - 1, at] = along(values, b)


def move_anchor(right, anchor, moved, per):
    along = mover(right, anchor.shape[1])
    for k, a in enumerate(range(STEP, DISP, STEP)):
        for at in blocks_of(per):
            moved[k, at] = along(anchor[at], -a)


def correlate(right, anchor, moved, other, shifted, c_high, c_low, per):
    columns = anchor.shape[1]
    along = mover(right, columns)
    column = lax.broadcasted_iota(jnp.int32, (8, columns), 1)
    place = jnp.where(right, columns - 1 - column, column)
    slab = 2 * GROUPS
    nothing = jnp.zeros((slab, columns), BF16)
    for c in (c_high, c_low):
        c[:slab] = nothing
        c[(DISP + 1) * slab :] = nothing
    blocks = blocks_of(per)
    for k, a in enumerate(range(0, DISP, STEP)):
        for i in range(0, len(blocks), 2):
            ours = [moved[k - 1, at] if k else anchor[at] for at in blocks[i : i + 2]]
            for b in range(min(STEP, DISP - a)):
                d = a + b
                tiles = []
                for m, at in zip(ours, blocks[i : i + 2]):
                    c = jnp.sum((m * (shifted[b - 1, at] if b else other[at])).reshape(per, 8, columns), axis=0)
                    c = along(c, a)
                    tiles.append(jnp.where(place >= d, c, 0.0) if d else c)
                high, low = split(jnp.concatenate(tiles, axis=0))
                at = slice((d + 1) * slab + i * 8, (d + 1) * slab + i * 8 + 16)
                c_high[at] = high
                c_low[at] = low


def filtered_pairs(half, banded, c_high, c_low):
    slab = 2 * GROUPS
    m = banded.shape[0] // 4
    weight = banded[pl.ds(pl.multiple_of(half * 2 * m, 2 * m), 2 * m)]
    for d in range(0, DISP, 2):
        at = [slice((d + k) * slab, (d + k + 3) * slab) for k in range(2)]
        high = jnp.concatenate([c_high[s] for s in at], axis=1)
        low = jnp.concatenate([c_low[s] for s in at], axis=1)
        y = mm(weight, high)
        yield d, y[:m] + (y[m:] + mm(weight[:m], low))


def near_kernel(flags, own, own_mate, partner, partner_mate, conv, lift, banded, part, anchor, other, moved, shifted, c_high, c_low):
    half = 1 - flags[1]
    right = flags[0] == 1
    per = lift.shape[0] // GROUPS
    fours = [four_rows(half, own, own_mate), four_rows(half, partner, partner_mate)]
    features(fours, conv, lift, [anchor, other], [rows_inside(flags, half)] * 2)
    move_anchor(right, anchor, moved, per)
    move_other(right, other, shifted, per)
    correlate(right, anchor, moved, other, shifted, c_high, c_low, per)
    for d, y in filtered_pairs(half, banded, c_high, c_low):
        part[d // 2] = y


def far_kernel(flags, own, own_far, partner, partner_far, conv, lift, banded, part, result, anchor, other, moved, shifted, c_high, c_low, out, sems):
    half = flags[1]
    right = flags[0] == 1
    per = lift.shape[0] // GROUPS
    fours = [four_rows(half, own, own_far), four_rows(half, partner, partner_far)]
    features(fours, conv, lift, [anchor, other], [rows_inside(flags, half)] * 2)
    move_other(right, other, shifted, per)
    move_anchor(right, anchor, moved, per)
    correlate(right, anchor, moved, other, shifted, c_high, c_low, per)
    columns = own.shape[2]
    outs = banded.shape[0] // 24
    rows = 2 * outs
    copies = []
    for d, y in filtered_pairs(half, banded, c_high, c_low):
        y = y + part[d // 2]
        for k in range(2):
            for row in range(2):
                o = from_columns(y[row * 3 * outs : (row + 1) * 3 * outs, k * columns : (k + 1) * columns], outs)
                out[pl.ds(row * outs * DISP + d + k, outs, stride=DISP)] = o
        if d + 2 in (DISP - LAST, DISP):
            i = len(copies)
            at = (slice(None), pl.ds(DISP - LAST, LAST) if i else pl.ds(0, DISP - LAST))
            copies.append(pltpu.make_async_copy(out.reshape(rows, DISP, columns).at[at], result.at[at], sems.at[i]))
            copies[-1].start()
    for copy in copies:
        copy.wait()


def vmem():
    return pl.BlockSpec(memory_space=pltpu.VMEM)


def smem():
    return pl.BlockSpec(memory_space=pltpu.SMEM)


def hbm():
    return pl.BlockSpec(memory_space=pltpu.HBM)


def call(kernel, name, out_shape, in_specs, scratch, *args, out_specs=None):
    return pl.pallas_call(
        kernel,
        out_shape=out_shape,
        in_specs=in_specs,
        out_specs=jax.tree.map(lambda _: vmem(), out_shape) if out_specs is None else out_specs,
        scratch_shapes=scratch,
        compiler_params=pltpu.CompilerParams(vmem_limit_bytes=VMEM_BYTES),
        cost_estimate=pl.CostEstimate(flops=COST, bytes_accessed=BYTES, transcendentals=0),
        name=name,
    )(*args)


def prepare(conv, lift, vol, mate):
    channels = conv.shape[2]
    feats = lift.shape[0]
    shapes = [(3 * channels, 9 * channels), (feats, 3 * channels), (8 * 3 * vol.shape[3], 6 * GROUPS)]
    out = [jax.ShapeDtypeStruct(s, BF16) for s in shapes]
    scratch = [pltpu.VMEM(x.shape, F32) for x in (conv, lift, vol)] + [pltpu.SemaphoreType.DMA((3,))]
    args = [pltpu.with_memory_space_constraint(x, pltpu.HBM) for x in (conv, lift, vol)]
    return call(prepare_kernel, "prepare", out, [hbm()] * 3 + [pl.BlockSpec(memory_space=pl.ANY)], scratch, *args, mate)


def sizes(operands, columns):
    feats = operands[1].shape[0]
    plain = (2 * feats, columns)
    moved = (-(-DISP // STEP) - 1, 2 * feats, columns)
    shifted = (STEP - 1, 2 * feats, columns)
    volume = ((DISP + 2) * 2 * GROUPS, columns)
    part = (DISP // 2, operands[2].shape[0] // 4, 2 * columns)
    return plain, moved, shifted, volume, part


def near(flags, own, own_mate, partner, partner_mate, operands):
    plain, moved, shifted, volume, part = sizes(operands, own.shape[2])
    scratch = [pltpu.VMEM(s, F32) for s in (plain, plain, moved, shifted)] + [pltpu.VMEM(volume, BF16)] * 2
    args = (own, own_mate, partner, partner_mate, *operands)
    out = jax.ShapeDtypeStruct(part, F32)
    return call(near_kernel, "near", out, [smem()] + [vmem()] * len(args), scratch, flags, *args)


def far(flags, own, own_far, partner, partner_far, operands, part):
    columns = own.shape[2]
    plain, moved, shifted, volume, _ = sizes(operands, columns)
    rows = operands[2].shape[0] // 12
    scratch = [pltpu.VMEM(s, F32) for s in (plain, plain, moved, shifted)] + [pltpu.VMEM(volume, BF16)] * 2
    scratch += [pltpu.VMEM((rows * DISP, columns), F32), pltpu.SemaphoreType.DMA((2,))]
    args = (own, own_far, partner, partner_far, *operands, part)
    in_specs = [smem()] + [vmem()] * len(args)
    out = jax.ShapeDtypeStruct((rows, DISP, columns), F32)
    return call(far_kernel, "far", out, in_specs, scratch, flags, *args, out_specs=hbm())


def routes(size):
    half, quarter = size // 2, size // 4

    def across(i):
        return (i + 1) % size if i % 2 else (i - 1) % size

    def apart(i, j):
        low, high = min(i, j), max(i, j)
        return high - low == 1 and high in (quarter, 3 * quarter)

    every = range(size)
    swap = [(i, (i + half) % size) for i in every]
    mates = [(i, i ^ 1) for i in every if not apart(i, i ^ 1)]
    far = [(across(i), i) for i in every if not apart(i, across(i))]
    far_partner = [((i + half) % size, j) for i, j in far]
    return swap, mates, far, far_partner


def on_device(images, conv_weight, lift_weight, vol_weight):
    size = lax.axis_size("rows")
    position = lax.axis_index("rows")
    quarter = size // 4
    swap, mates, beyond, beyond_partner = routes(size)
    starts = (position == quarter) | (position == 3 * quarter)
    ends = (position == quarter - 1) | (position == 3 * quarter - 1)
    right = (position < quarter) | (position >= 3 * quarter)
    flags = jnp.stack([jnp.where(right, 1, 0), position % 2, jnp.where(starts, 0, 1), jnp.where(ends, 0, 1)]).astype(jnp.int32)

    partner = lax.ppermute(images, "rows", swap)
    partner_far = lax.ppermute(images, "rows", beyond_partner)
    own_mate = lax.ppermute(images, "rows", mates)
    own_far = lax.ppermute(images, "rows", beyond)
    partner_mate = lax.ppermute(partner, "rows", mates)
    operands = prepare(conv_weight, lift_weight, vol_weight, own_mate)
    part = near(flags, images, own_mate, partner, partner_mate, operands)
    whole = far(flags, images, own_far, partner, partner_far, operands, part)
    rows, _, columns = images.shape
    return whole.reshape(rows, vol_weight.shape[3], DISP, columns)


def solution(mesh):
    return jax.shard_map(
        on_device,
        mesh=mesh,
        in_specs=(P(("scenes", "rows"), None, None), P(), P(), P()),
        out_specs=P(("scenes", "rows"), None, None, None),
        check_vma=False,
    )
```
